512 devices in a mesh: dp: 8 (over x, core), seq: 64 (over y, z).
Axes of the slice: x: 4, y: 8, z: 8, core: 2. Of those that a mesh axis runs over, the one named last changes fastest.
Arguments:
- queries: bfloat16 [8, 8192, 1024], P('dp', 'seq'), may hold values from -6 to 6
- keys: bfloat16 [8, 8192, 1024], P('dp', 'seq'), may hold values from -6 to 6
- values: bfloat16 [8, 8192, 1024], P('dp', 'seq'), may hold values from -6 to 6
- cotangent: bfloat16 [8, 8192, 1024], P('dp', 'seq'), may hold values from -6 to 6
- out_weight: bfloat16 [1024, 1024], P('dp'), may hold values from -0.1875 to 0.1875
Outputs:
- output: bfloat16 [8, 8192, 1024], P('dp', 'seq')
- grad_queries: bfloat16 [8, 8192, 1024], P('dp', 'seq')
- grad_keys: bfloat16 [8, 8192, 1024], P('dp', 'seq')
- grad_values: bfloat16 [8, 8192, 1024], P('dp', 'seq')
- grad_weight: float32 [1024, 1024], P(('dp', 'seq'))
The draws below stay inside these ranges and needn't reach their ends.
All inputs are finite; a program needn't handle non-finite values.
Results may differ from the reference program's by a relative error of at most 0.015.
Values may be sent and summed in bfloat16 or wider, within the bound.
A program may use at most 128 MiB of HBM per device.

```python
import math
import jax
import jax.numpy as jnp
from jax import lax

HEADS = 8
DH = 128
E = 1024
TOK_DEV = 128
F = 1024
LEN = 8192
SEQS = 8


def shard_levels(key, dims, cuts, least, top_value):
    factor_of, own = 1.0, jax.random.fold_in(key, 6)
    for axis_at, shards_of in cuts:
        steps = jnp.exp(jax.random.uniform(jax.random.fold_in(own, axis_at), (shards_of,), jnp.float32, least / len(cuts), top_value / len(cuts)))
        factor_of = factor_of * jnp.repeat(steps, dims[axis_at] // shards_of).reshape([-1 if axis == axis_at else 1 for axis in range(len(dims))])
    return factor_of


def bell_draw(key, dims, spread, reach, shards=(), held_as=jnp.bfloat16):
    factor_of = shard_levels(key, dims, shards, -0.22, 0.18) if shards else 1.0
    entries = jax.random.normal(key, dims, jnp.float32) * spread * factor_of
    return jnp.minimum(jnp.maximum(entries, -reach), reach).astype(held_as)


def setup_inputs(seed: int = 0) -> dict:
    key_of = jax.random.split(jax.random.key(seed), 6)
    queries = bell_draw(key_of[0], (SEQS, LEN, F), 1.0, 6.0, ((0, 8), (1, 64)))
    keys = bell_draw(key_of[1], (SEQS, LEN, F), 1.0, 6.0, ((0, 8), (1, 64)))
    values = bell_draw(key_of[2], (SEQS, LEN, F), 1.0, 6.0, ((0, 8), (1, 64)))
    cotangent = bell_draw(key_of[3], (SEQS, LEN, E), 1.0, 6.0, ((0, 8), (1, 64)))
    out_weight = bell_draw(key_of[4], (E, F), F ** -0.5, 0.1875, ((0, 8),))
    return dict(queries=queries, keys=keys, values=values, cotangent=cotangent, out_weight=out_weight)


epsilon = 1e-05

def rounded(values):
    return lax.optimization_barrier(values.astype(jnp.bfloat16)).astype(jnp.float32)

def sequence_pass(queries, keys, values, cotangent, out_weight):
    blocks = LEN // TOK_DEV
    shape = (blocks, TOK_DEV, HEADS, DH)
    query_f = queries.reshape(shape).astype(jnp.float32)
    key_f = keys.reshape(shape).astype(jnp.float32)
    value_f = values.reshape(shape).astype(jnp.float32)
    causal = jnp.tril(jnp.ones((TOK_DEV, TOK_DEV), dtype=jnp.bool_))
    scores = jnp.einsum('bthd,bshd->bhts', query_f, key_f)
    attend = rounded(jnp.where(causal, scores, jnp.float32(0.0)))
    local_kv = jnp.einsum('bshd,bshe->bhde', key_f, value_f)
    totals = jnp.cumsum(local_kv, axis=0)
    prior = jnp.concatenate([jnp.zeros_like(local_kv[:1]), totals[:-1]], axis=0)
    mixed = jnp.einsum('bhts,bshd->bthd', attend, value_f)
    mixed = mixed + jnp.einsum('bthd,bhde->bthe', query_f, prior, precision=lax.Precision.HIGHEST)
    root_mean = jnp.sqrt(lax.optimization_barrier(jnp.mean(mixed * mixed, axis=-1, keepdims=True)) + epsilon)
    normed = mixed / root_mean
    normed_rows = normed.astype(jnp.bfloat16).reshape(LEN, F)
    output = jnp.dot(normed_rows, out_weight.T, preferred_element_type=jnp.float32).astype(jnp.bfloat16)
    dnormed = jnp.dot(cotangent, out_weight, preferred_element_type=jnp.float32).reshape(shape)
    dmixed = (dnormed - normed * lax.optimization_barrier(jnp.mean(dnormed * normed, axis=-1, keepdims=True))) / root_mean
    dmixed_f = rounded(dmixed)
    local_u = jnp.einsum('bthd,bthe->bhde', query_f, dmixed_f)
    suffix = jnp.cumsum(local_u[::-1], axis=0)[::-1]
    later = jnp.concatenate([suffix[1:], jnp.zeros_like(local_u[:1])], axis=0)
    back = rounded(jnp.where(causal, jnp.einsum('bthe,bshe->bhts', dmixed_f, value_f), jnp.float32(0.0)))
    grad_q = jnp.einsum('bhts,bshd->bthd', back, key_f)
    grad_q = grad_q + jnp.einsum('bthe,bhde->bthd', dmixed_f, prior, precision=lax.Precision.HIGHEST)
    grad_k = jnp.einsum('bhts,bthd->bshd', back, query_f)
    grad_k = grad_k + jnp.einsum('bshe,bhde->bshd', value_f, later, precision=lax.Precision.HIGHEST)
    grad_v = jnp.einsum('bhts,bthe->bshe', attend, dmixed_f)
    grad_v = grad_v + jnp.einsum('bshd,bhde->bshe', key_f, later, precision=lax.Precision.HIGHEST)
    partial_grad = jnp.dot(cotangent.T, normed_rows, preferred_element_type=jnp.float32)
    return (output, grad_q.reshape(LEN, F).astype(jnp.bfloat16), grad_k.reshape(LEN, F).astype(jnp.bfloat16), grad_v.reshape(LEN, F).astype(jnp.bfloat16), partial_grad)

def reference(queries, keys, values, cotangent, out_weight):

    def one_sequence(items):
        return sequence_pass(items[0], items[1], items[2], items[3], out_weight)
    output, grad_queries, grad_keys, grad_values, partials = lax.map(one_sequence, (queries, keys, values, cotangent))
    grad_weight = lax.optimization_barrier(jnp.sum(partials, axis=0)) * (1.0 / math.sqrt(SEQS * LEN))
    return (output, grad_queries, grad_keys, grad_values, grad_weight)
```

```python
import functools
import math

import jax
import jax.numpy as jnp
from jax import lax
from jax.experimental import pallas as pl
from jax.experimental.pallas import tpu as pltpu
from jax.sharding import PartitionSpec as P

MESH = pl.DeviceIdType.MESH
DH = 128
EPSILON = 1e-05
BF16 = jnp.bfloat16
F32 = jnp.float32


def dot(left, right, contract):
    return lax.dot_general(left, right, ((contract[:1], contract[1:]), ((), ())), preferred_element_type=F32)


def head_cols(h):
    return pl.ds(pl.multiple_of(h * DH, DH), DH)


def kernel(
    sizes,
    q_hbm, k_hbm, v_hbm, c_hbm, w_hbm,
    out_hbm, gq_hbm, gk_hbm, gv_hbm, gw_hbm,
    q, k, v, c, wall, dn,
    a_send, a_recv, p_send, prior,
    b_send, b_recv, l_send, later,
    attend, part, normed, dmixed, nall, ccol, ccolt,
    gk_part, gv_part, g_tile, g_rows, g_send, g_recv,
    out_v, gq_v, gk_v, gv_v, gw_v,
    load_sem, store_sem, send_sem, a_sem, p_sem, b_sem, l_sem, g_sem,
    w_sem, c_sem, n_sem,
):
    dps, ny, nz, heads = sizes
    nx = dps // 2
    seqs = ny * nz
    block = q.shape[0]
    me_dp, me = lax.axis_index("dp"), lax.axis_index("seq")
    x, core = me_dp // 2, me_dp % 2
    y, z = me // nz, me % nz
    right = ((x + 1) % nx) * 2 + core
    left = ((x + nx - 1) % nx) * 2 + core
    sibling = x * 2 + (1 - core)
    opposite = ((x + 2) % nx) * 2 + core
    right_s = ((x + 1) % nx) * 2 + (1 - core)
    left_s = ((x + nx - 1) % nx) * 2 + (1 - core)
    opposite_s = ((x + 2) % nx) * 2 + (1 - core)

    def turn(i):
        return (ny + (2 * (i % 2) - 1) * ((i + 1) // 2)) % ny

    barrier = pltpu.get_barrier_semaphore()

    def greet_seq(i, carry):
        pl.semaphore_signal(barrier, inc=1, device_id=(me_dp, (me + i) % seqs), device_id_type=MESH)
        return carry

    def greet_dp(i, carry):
        pl.semaphore_signal(barrier, inc=1, device_id=((me_dp + i) % dps, me), device_id_type=MESH)
        return carry

    loads = [
        pltpu.make_async_copy(src, dst, load_sem.at[i])
        for i, (src, dst) in enumerate(
            [(k_hbm, k), (v_hbm, v), (w_hbm, wall.at[me_dp]), (c_hbm, c), (q_hbm, q)]
        )
    ]
    for load in loads:
        load.start()
    lax.fori_loop(1, seqs, greet_seq, 0)
    lax.fori_loop(1, dps, greet_dp, 0)

    loads[0].wait()
    loads[1].wait()

    def local_state(h, carry):
        kv = dot(k[:, head_cols(h)], v[:, head_cols(h)], (0, 0))
        a_send[pl.ds(h * 8, 8)] = kv.astype(BF16).reshape(8, 16, DH)
        return carry

    lax.fori_loop(0, heads, local_state, 0)
    a_recv[me] = a_send[me]
    loads[2].wait()
    pl.semaphore_wait(barrier, seqs - 1 + dps - 1)

    def remote(src, dst, send, recv, dp, seq):
        return pltpu.make_async_remote_copy(
            src_ref=src, dst_ref=dst, send_sem=send, recv_sem=recv, device_id=(dp, seq), device_id_type=MESH
        )

    def arrived(ref, sem):
        remote(ref, ref, send_sem.at[0], sem, sibling, me).wait_recv()

    W_LEFT, W_RIGHT, W_OPP0, W_OPP1, W_SIB, W_SIB_LEFT, W_SIB_RIGHT, W_SIB_OPP = range(8)
    half = block // 2
    own_w = wall.at[me_dp]
    remote(own_w, own_w, send_sem.at[0], w_sem.at[W_LEFT], right, me).start()
    remote(own_w, own_w, send_sem.at[0], w_sem.at[W_RIGHT], left, me).start()
    remote(own_w, own_w, send_sem.at[0], w_sem.at[W_SIB], sibling, me).start()

    def scatter(source, landing, send, recv):
        def one(i, carry):
            target = ((y + turn(i // nz)) % ny) * nz + (z + i) % nz
            remote(source.at[target], landing.at[me], send, recv, me_dp, target).start()
            return carry

        lax.fori_loop(1, seqs, one, 0)

    scatter(a_send, a_recv, send_sem.at[1], a_sem)

    loads[3].wait()
    ccol[me_dp] = c[:, head_cols(me_dp)]

    def send_columns(i, carry):
        target = (me_dp + i) % dps
        remote(c.at[:, head_cols(target)], ccol.at[me_dp], send_sem.at[2], c_sem, target, me).start()
        return carry

    lax.fori_loop(1, dps, send_columns, 0)

    loads[4].wait()
    causal = lax.broadcasted_iota(jnp.int32, (block, block), 0) >= lax.broadcasted_iota(
        jnp.int32, (block, block), 1
    )

    def within(h, carry):
        scores = dot(q[:, head_cols(h)], k[:, head_cols(h)], (1, 1))
        near = jnp.where(causal, scores, 0.0).astype(BF16)
        attend[h] = near
        part[h] = dot(near, v[:, head_cols(h)], (1, 0))
        return carry

    lax.fori_loop(0, heads, within, 0)

    arrived(a_recv.at[pl.ds(0, seqs - 1)], a_sem)

    def forward_sum(s, total):
        p_send[s] = total.astype(BF16)
        return total + a_recv[s].astype(F32)

    lax.fori_loop(0, seqs, forward_sum, jnp.zeros((16, DH), F32))
    prior[me] = p_send[me]

    def give_back(source, landing, send, recv):
        def one(i, carry):
            target = ((y + turn(i // nz)) % ny) * nz + (z + i) % nz
            remote(source.at[target], landing.at[me], send, recv.at[y], me_dp, target).start()
            return carry

        lax.fori_loop(1, seqs, one, 0)

    give_back(p_send, prior, send_sem.at[3], p_sem)

    from_left, from_right = wall.at[left], wall.at[right]
    arrived(from_left, w_sem.at[W_LEFT])
    low, high = pl.ds(0, half), pl.ds(half, half)
    remote(from_left.at[low], from_left.at[low], send_sem.at[0], w_sem.at[W_OPP0], right, me).start()
    remote(from_left, from_left, send_sem.at[0], w_sem.at[W_SIB_LEFT], sibling, me).start()
    arrived(from_right, w_sem.at[W_RIGHT])
    remote(from_right.at[high], from_right.at[high], send_sem.at[0], w_sem.at[W_OPP1], left, me).start()
    remote(from_right, from_right, send_sem.at[0], w_sem.at[W_SIB_RIGHT], sibling, me).start()

    dn[...] = jnp.zeros_like(dn)

    def add_rows(d):
        dn[...] += dot(c[:, head_cols(d)], wall[d], (1, 0))

    add_rows(me_dp)
    add_rows(left)
    add_rows(right)
    arrived(wall.at[sibling], w_sem.at[W_SIB])
    add_rows(sibling)
    arrived(wall.at[opposite, low], w_sem.at[W_OPP0])
    arrived(wall.at[opposite, high], w_sem.at[W_OPP1])
    remote(wall.at[opposite], wall.at[opposite], send_sem.at[0], w_sem.at[W_SIB_OPP], sibling, me).start()
    add_rows(opposite)
    arrived(wall.at[left_s], w_sem.at[W_SIB_LEFT])
    add_rows(left_s)
    arrived(wall.at[right_s], w_sem.at[W_SIB_RIGHT])
    add_rows(right_s)
    arrived(wall.at[opposite_s], w_sem.at[W_SIB_OPP])
    add_rows(opposite_s)

    N_LEFT, N_RIGHT, N_OPP0, N_OPP1, N_SIB, N_SIB_LEFT, N_SIB_RIGHT, N_SIB_OPP = range(8)

    def middle(h, first):
        mixed = part[h] + dot(q[:, head_cols(h)], prior[pl.ds(h * 8, 8)].reshape(DH, DH), (1, 0))
        inverse = lax.rsqrt(jnp.mean(mixed * mixed, axis=-1, keepdims=True) + EPSILON)
        n = mixed * inverse
        dnormed = dn[:, head_cols(h)]
        dmix = (dnormed - n * jnp.mean(dnormed * n, axis=-1, keepdims=True)) * inverse
        dmix = dmix.astype(BF16)
        u = dot(q[:, head_cols(h)], dmix, (0, 0))
        b_send[pl.ds(h * 8, 8)] = u.astype(BF16).reshape(8, 16, DH)
        dmixed[h] = dmix
        n = n.astype(BF16)
        nall[h, me_dp] = n
        normed[:, head_cols(h)] = n

        def one(i, carry):
            target = h * nz + (z + i) % nz
            remote(b_send.at[target], b_recv.at[me], send_sem.at[4], b_sem, me_dp, target).start()
            return carry

        lax.fori_loop(1 if first else 0, nz, one, 0)
        own_n = nall.at[h, me_dp]
        remote(own_n, own_n, send_sem.at[5], n_sem.at[N_LEFT], right, me).start()
        remote(own_n, own_n, send_sem.at[5], n_sem.at[N_RIGHT], left, me).start()
        remote(own_n, own_n, send_sem.at[5], n_sem.at[N_SIB], sibling, me).start()

    arrived(prior.at[pl.ds(0, nz - 1)], p_sem.at[y])
    middle(y, True)
    b_recv[me] = b_send[me]

    def other_heads(i, carry):
        h = (y + ny - turn(i)) % ny
        arrived(prior.at[pl.ds(h * 8, 8)], p_sem.at[h])
        middle(h, False)
        return carry

    lax.fori_loop(1, heads, other_heads, 0)

    def within_back(h, carry):
        cols = head_cols(h)
        dmix = dmixed[h]
        back = jnp.where(causal, dot(dmix, v[:, cols], (1, 1)), 0.0).astype(BF16)
        grad_q = dot(back, k[:, cols], (1, 0)) + dot(dmix, prior[pl.ds(h * 8, 8)].reshape(DH, DH), (1, 1))
        gq_v[:, cols] = grad_q.astype(BF16)
        gk_part[h] = dot(back, q[:, cols], (0, 0))
        gv_part[h] = dot(attend[h], dmix, (0, 0))
        return carry

    lax.fori_loop(0, heads, within_back, 0)
    stores = [pltpu.make_async_copy(gq_v, gq_hbm, store_sem.at[0])]
    stores[0].start()

    arrived(b_recv.at[pl.ds(0, seqs - 1)], b_sem)

    def backward_sum(i, total):
        s = seqs - 1 - i
        l_send[s] = total.astype(BF16)
        return total + b_recv[s].astype(F32)

    lax.fori_loop(0, seqs, backward_sum, jnp.zeros((16, DH), F32))
    later[me] = l_send[me]
    give_back(l_send, later, send_sem.at[6], l_sem)

    lower, upper = pl.ds(0, heads // 2), pl.ds(heads // 2, heads // 2)

    def arrived_heads(who, sem, count=heads):
        remote(nall.at[0, pl.ds(0, count)], nall.at[0, pl.ds(0, count)], send_sem.at[0], sem, who, me).wait_recv()

    def pass_on(who, sem, to, first, count):
        def one(h, carry):
            there = nall.at[h, who]
            remote(there, there, send_sem.at[5], sem, to, me).start()
            return carry

        lax.fori_loop(first, first + count, one, 0)

    arrived_heads(left, n_sem.at[N_LEFT])
    pass_on(left, n_sem.at[N_OPP0], right, 0, heads // 2)
    pass_on(left, n_sem.at[N_SIB_LEFT], sibling, 0, heads)
    arrived_heads(right, n_sem.at[N_RIGHT])
    pass_on(right, n_sem.at[N_OPP1], left, heads // 2, heads // 2)
    pass_on(right, n_sem.at[N_SIB_RIGHT], sibling, 0, heads)

    def project(d, carry):
        out_v[:, head_cols(d)] = dot(normed[...], wall[d], (1, 1)).astype(BF16)
        return carry

    lax.fori_loop(0, dps, project, 0)
    stores.append(pltpu.make_async_copy(out_v, out_hbm, store_sem.at[1]))
    stores[1].start()

    arrived(ccol.at[pl.ds(0, dps - 1)], c_sem)

    def transpose(d, carry):
        ccolt[:, head_cols(d)] = ccol[d].T
        return carry

    lax.fori_loop(0, dps, transpose, 0)

    arrived_heads(opposite, n_sem.at[N_OPP0], heads // 2)
    arrived_heads(opposite, n_sem.at[N_OPP1], heads // 2)
    pass_on(opposite, n_sem.at[N_SIB_OPP], sibling, 0, heads)
    arrived_heads(sibling, n_sem.at[N_SIB])
    arrived_heads(left_s, n_sem.at[N_SIB_LEFT])
    arrived_heads(right_s, n_sem.at[N_SIB_RIGHT])
    arrived_heads(opposite_s, n_sem.at[N_SIB_OPP])

    factor = 1.0 / math.sqrt(dps * block * seqs)

    def weight_rows(h, carry):
        g_tile[...] = dot(ccolt[...], nall[h].reshape(dps * block, DH), (1, 0)) * factor
        for r in range(2):
            g_rows[pl.ds(2 * h + r, seqs, stride=16), :] = g_tile[pl.ds(r, seqs, stride=2), :]
        return carry

    lax.fori_loop(0, heads, weight_rows, 0)

    def round_rows(s, carry):
        g_send[s] = g_rows[pl.ds(pl.multiple_of(s * 16, 16), 16), :].astype(BF16)
        return carry

    lax.fori_loop(0, seqs, round_rows, 0)
    g_recv[me] = g_send[me]
    scatter(g_send, g_recv, send_sem.at[7], g_sem)

    def finish(h):
        cols = head_cols(h)
        state = later[pl.ds(h * 8, 8)].reshape(DH, DH)
        gk_v[:, cols] = (gk_part[h] + dot(v[:, cols], state, (1, 1))).astype(BF16)
        gv_v[:, cols] = (gv_part[h] + dot(k[:, cols], state, (1, 0))).astype(BF16)

    arrived(later.at[pl.ds(0, nz - 1)], l_sem.at[y])
    finish(y)

    def finish_others(i, carry):
        h = (y + ny - turn(i)) % ny
        arrived(later.at[pl.ds(h * 8, 8)], l_sem.at[h])
        finish(h)
        return carry

    lax.fori_loop(1, heads, finish_others, 0)
    stores.append(pltpu.make_async_copy(gk_v, gk_hbm, store_sem.at[2]))
    stores.append(pltpu.make_async_copy(gv_v, gv_hbm, store_sem.at[3]))
    stores[2].start()
    stores[3].start()

    arrived(g_recv.at[pl.ds(0, seqs - 1)], g_sem)
    total = lax.fori_loop(0, seqs, lambda s, t: t + g_recv[s].astype(F32), jnp.zeros((16, DH), F32))
    for h in range(heads):
        gw_v[:, h * DH : (h + 1) * DH] = total[2 * h : 2 * h + 2]
    stores.append(pltpu.make_async_copy(gw_v, gw_hbm, store_sem.at[4]))
    stores[4].start()

    def sent(ref, i):
        remote(ref, ref, send_sem.at[i], a_sem, sibling, me).wait_send()

    sent(wall.at[pl.ds(0, 7)], 0)
    sent(a_send.at[pl.ds(0, seqs - 1)], 1)
    sent(ccol.at[pl.ds(0, dps - 1)], 2)
    sent(p_send.at[pl.ds(0, seqs - 1)], 3)
    sent(b_send.at[pl.ds(0, seqs - 1)], 4)
    sent(nall.at[pl.ds(0, 7)], 5)
    sent(l_send.at[pl.ds(0, seqs - 1)], 6)
    sent(g_send.at[pl.ds(0, seqs - 1)], 7)
    for store in stores:
        store.wait()


def local(sizes, queries, keys, values, cotangent, out_weight):
    dps, ny, nz, heads = sizes
    _, block, features = queries.shape
    seqs = ny * nz
    rows = jax.ShapeDtypeStruct((block, features), BF16)
    states = pltpu.VMEM((seqs, 16, DH), BF16)
    whole = pltpu.VMEM((block, features), BF16)
    per_head = pltpu.VMEM((heads, block, DH), F32)
    dma = pltpu.SemaphoreType.DMA
    out = pl.pallas_call(
        functools.partial(kernel, sizes),
        out_shape=[rows] * 4 + [jax.ShapeDtypeStruct((2, features), F32)],
        in_specs=[pl.BlockSpec(memory_space=pl.ANY)] * 5,
        out_specs=[pl.BlockSpec(memory_space=pl.ANY)] * 5,
        scratch_shapes=[
            whole, whole, whole, whole,
            pltpu.VMEM((dps, block, features), BF16),
            pltpu.VMEM((block, features), F32),
            states, states, states, states,
            states, states, states, states,
            pltpu.VMEM((heads, block, block), BF16),
            per_head,
            whole,
            pltpu.VMEM((heads, block, DH), BF16),
            pltpu.VMEM((heads, dps, block, DH), BF16),
            pltpu.VMEM((dps, block, DH), BF16),
            pltpu.VMEM((DH, dps * block), BF16),
            per_head, per_head,
            pltpu.VMEM((block, DH), F32),
            pltpu.VMEM((seqs * 16, DH), F32),
            states, states,
            whole, whole, whole, whole,
            pltpu.VMEM((2, features), F32),
            dma((5,)), dma((5,)), dma((8,)), dma, dma((heads,)), dma, dma((heads,)), dma,
            dma((8,)), dma, dma((8,)),
        ],
        compiler_params=pltpu.CompilerParams(
            collective_id=0, has_side_effects=True, vmem_limit_bytes=40 * 1024 * 1024
        ),
    )(queries[0], keys[0], values[0], cotangent[0], out_weight)
    return tuple(part[None] for part in out[:4]) + (out[4],)


def solution(mesh):
    seqs = mesh.shape["seq"]
    ny = nz = math.isqrt(seqs)
    sizes = (mesh.shape["dp"], ny, nz, 8)
    tokens = P("dp", "seq", None)
    return jax.shard_map(
        functools.partial(local, sizes),
        mesh=mesh,
        in_specs=(tokens, tokens, tokens, tokens, P("dp", None)),
        out_specs=(tokens, tokens, tokens, tokens, P(("dp", "seq"), None)),
        check_vma=False,
    )
```

```python
import functools
import math

import jax
import jax.numpy as jnp
from jax import lax
from jax.experimental import pallas as pl
from jax.experimental.pallas import tpu as pltpu
from jax.sharding import PartitionSpec as P

MESH = pl.DeviceIdType.MESH
DH = 128
EPSILON = 1e-05
BF16 = jnp.bfloat16
F32 = jnp.float32
VMEM_LIMIT = 40 * 1024 * 1024


def dot(left, right, contract):
    return lax.dot_general(left, right, ((contract[:1], contract[1:]), ((), ())), preferred_element_type=F32)


def head_cols(h):
    return pl.ds(pl.multiple_of(h * DH, DH), DH)


def far_first(count):
    return sorted(range(count), key=lambda d: -min(d, count - d))


def kernel(
    sizes,
    q_hbm, k_hbm, v_hbm, c_hbm, w_hbm,
    out_hbm, gq_hbm, gk_hbm, gv_hbm, gw_hbm,
    q, k, v, c, wall, dn,
    a_send, a_recv, p_send, prior,
    b_send, b_recv, l_send, later,
    attend, part, normed, dmixed, n_send, nall, ccol, ccolt,
    gk_part, gv_part, g_tile, g_rows, g_send, g_recv, g_sum, g_other,
    out_v, gq_v, gk_v, gv_v, gw_v,
    load_sem, store_sem, send_sem, a_sem, p_sem, b_sem, l_sem, g_sem,
    w_sem, c_sem, n_sem, swap_sem,
):
    dps, ny, nz, heads = sizes
    nx = dps // 2
    seqs = ny * nz
    block = q.shape[0]
    half = block // 2
    me_dp, me = lax.axis_index("dp"), lax.axis_index("seq")
    x, core = me_dp // 2, me_dp % 2
    y, z = me // nz, me % nz
    x_right, x_left, x_opposite = (x + 1) % nx, (x + nx - 1) % nx, (x + 2) % nx
    other = 1 - core
    right, left, opposite = x_right * 2 + core, x_left * 2 + core, x_opposite * 2 + core
    sibling = x * 2 + other
    right_s, left_s, opposite_s = x_right * 2 + other, x_left * 2 + other, x_opposite * 2 + other

    y_order, z_order = far_first(ny), far_first(nz)
    columns = [(z + d) % nz for d in z_order]

    def row_at(i):
        step = (ny - i) // 2
        sign = 2 * (i % 2) - 1
        return (y + ny + sign * step) % ny

    def each_other(act):
        def rows(i, carry):
            base = row_at(i) * nz
            for column in columns:
                act(base + column)
            return carry

        lax.fori_loop(0, ny - 1, rows, 0)
        for column in columns[:-1]:
            act(y * nz + column)

    loads = [
        pltpu.make_async_copy(src, dst, load_sem.at[i])
        for i, (src, dst) in enumerate(
            [(k_hbm, k), (v_hbm, v), (w_hbm, wall.at[me_dp]), (q_hbm, q), (c_hbm, c)]
        )
    ]
    for load in loads:
        load.start()

    barrier = pltpu.get_barrier_semaphore()

    def greet(dp, seq):
        pl.semaphore_signal(barrier, inc=1, device_id=(dp, seq), device_id_type=MESH)

    each_other(lambda seq: greet(me_dp, seq))
    for dp in (opposite, opposite_s, right, left, right_s, left_s, sibling):
        greet(dp, me)

    loads[0].wait()
    loads[1].wait()
    for h in range(heads):
        cols = slice(h * DH, (h + 1) * DH)
        a_send[h * 8 : h * 8 + 8] = dot(k[:, cols], v[:, cols], (0, 0)).astype(BF16).reshape(8, 16, DH)
    a_recv[me] = a_send[me]
    loads[2].wait()
    pl.semaphore_wait(barrier, seqs - 1 + dps - 1)

    def remote(src, dst, send, recv, dp, seq):
        return pltpu.make_async_remote_copy(
            src_ref=src, dst_ref=dst, send_sem=send, recv_sem=recv, device_id=(dp, seq), device_id_type=MESH
        )

    def send(ref, group, recv, dp):
        remote(ref, ref, send_sem.at[group], recv, dp, me).start()

    def arrived(ref, sem):
        remote(ref, ref, send_sem.at[0], sem, sibling, me).wait_recv()

    def exchange(source, landing, group, recv):
        each_other(lambda seq: remote(source.at[seq], landing.at[me], send_sem.at[group], recv, me_dp, seq).start())

    W_LEFT0, W_LEFT1, W_RIGHT0, W_RIGHT1, W_OPP0, W_OPP1, W_SIB, W_SIB_LEFT, W_SIB_RIGHT, W_SIB_OPP = range(10)
    low, high = pl.ds(0, half), pl.ds(half, half)
    send(wall.at[me_dp, low], 0, w_sem.at[W_LEFT0], right)
    send(wall.at[me_dp, high], 0, w_sem.at[W_RIGHT1], left)
    exchange(a_send, a_recv, 1, a_sem)
    send(wall.at[me_dp, high], 0, w_sem.at[W_LEFT1], right)
    send(wall.at[me_dp, low], 0, w_sem.at[W_RIGHT0], left)
    send(wall.at[me_dp], 0, w_sem.at[W_SIB], sibling)

    loads[3].wait()
    causal = lax.broadcasted_iota(jnp.int32, (block, block), 0) >= lax.broadcasted_iota(
        jnp.int32, (block, block), 1
    )
    for h in range(heads):
        cols = slice(h * DH, (h + 1) * DH)
        near = jnp.where(causal, dot(q[:, cols], k[:, cols], (1, 1)), 0.0).astype(BF16)
        attend[h] = near
        part[h] = dot(near, v[:, cols], (1, 0))

    arrived(wall.at[left, low], w_sem.at[W_LEFT0])
    send(wall.at[left, low], 0, w_sem.at[W_OPP0], right)
    arrived(wall.at[right, high], w_sem.at[W_RIGHT1])
    send(wall.at[right, high], 0, w_sem.at[W_OPP1], left)

    arrived(a_recv.at[pl.ds(0, seqs - 1)], a_sem)

    def forward_sum(s, total):
        p_send[s] = total.astype(BF16)
        return total + a_recv[s].astype(F32)

    lax.fori_loop(0, seqs, forward_sum, jnp.zeros((16, DH), F32), unroll=8)
    prior[me] = p_send[me]
    exchange(p_send, prior, 3, p_sem.at[y])

    arrived(wall.at[left, high], w_sem.at[W_LEFT1])
    send(wall.at[left], 0, w_sem.at[W_SIB_LEFT], sibling)
    arrived(wall.at[right, low], w_sem.at[W_RIGHT0])
    send(wall.at[right], 0, w_sem.at[W_SIB_RIGHT], sibling)
    arrived(wall.at[opposite, low], w_sem.at[W_OPP0])
    arrived(wall.at[opposite, high], w_sem.at[W_OPP1])
    send(wall.at[opposite], 0, w_sem.at[W_SIB_OPP], sibling)

    C_FAR, C_SIB = range(2)
    wide = 2 * DH

    def chip_cols(chip):
        return pl.ds(pl.multiple_of(chip * wide, wide), wide)

    loads[4].wait()
    for chip, dp in ((x_opposite, opposite), (x_right, right), (x_left, left)):
        remote(c.at[:, chip_cols(chip)], ccol.at[x, core], send_sem.at[2], c_sem.at[C_FAR], dp, me).start()
    ccol[x, core] = c[:, chip_cols(x)]

    arrived(wall.at[sibling], w_sem.at[W_SIB])
    arrived(wall.at[left_s], w_sem.at[W_SIB_LEFT])
    arrived(wall.at[right_s], w_sem.at[W_SIB_RIGHT])
    arrived(wall.at[opposite_s], w_sem.at[W_SIB_OPP])
    dn[...] = dot(c[...], wall[...].reshape(dps * block, heads * DH), (1, 0))

    N_LEFT0, N_LEFT1, N_RIGHT0, N_RIGHT1, N_OPP0, N_OPP1, N_SIB = range(7)
    pairs = heads // 2

    def middle(h):
        mixed = part[h] + dot(q[:, head_cols(h)], prior[pl.ds(h * 8, 8)].reshape(DH, DH), (1, 0))
        inverse = lax.rsqrt(jnp.mean(mixed * mixed, axis=-1, keepdims=True) + EPSILON)
        n = mixed * inverse
        dnormed = dn[:, head_cols(h)]
        dmix = (dnormed - n * jnp.mean(dnormed * n, axis=-1, keepdims=True)) * inverse
        dmix = dmix.astype(BF16)
        b_send[pl.ds(h * 8, 8)] = dot(q[:, head_cols(h)], dmix, (0, 0)).astype(BF16).reshape(8, 16, DH)
        dmixed[h] = dmix
        n = n.astype(BF16)
        n_send[h] = n
        normed[:, head_cols(h)] = n

    def send_states(h, own):
        for column in columns[:-1] if own else columns:
            target = h * nz + column
            remote(b_send.at[target], b_recv.at[me], send_sem.at[4], b_sem, me_dp, target).start()

    def send_normed(h):
        taker = h % 2

        def give(recv, dp):
            remote(n_send.at[h], nall.at[h // 2, me_dp], send_sem.at[5], recv, dp, me).start()

        give(n_sem.at[N_LEFT0 + core, h // 2], x_right * 2 + taker)
        give(n_sem.at[N_RIGHT0 + core, h // 2], x_left * 2 + taker)

        @pl.when(taker == other)
        def _():
            give(n_sem.at[N_SIB, 0], sibling)

    arrived(prior.at[pl.ds(0, nz - 1)], p_sem.at[y])
    near_rows = [(y + d) % ny for d in y_order[:-1][::-1]]
    group = [y] + near_rows[:3]
    for h in group[1:]:
        arrived(prior.at[pl.ds(h * 8, 8)], p_sem.at[h])
    for h in group:
        middle(h)
    b_recv[me] = b_send[me]
    for h in group[:0:-1]:
        send_states(h, False)
    send_states(y, True)
    for h in group:
        send_normed(h)
    group = near_rows[:2:-1]
    for h in group:
        arrived(prior.at[pl.ds(h * 8, 8)], p_sem.at[h])
    for h in group:
        middle(h)
    for h in group:
        send_states(h, False)
    for h in group:
        send_normed(h)

    for i in range(pairs):
        nall[i, me_dp] = n_send[2 * i + core]

    def arrived_columns(chips, sem):
        arrived(ccol.at[pl.ds(0, chips), 0], sem)

    arrived_columns(nx - 1, c_sem.at[C_FAR])
    for chip in range(nx):
        send(ccol.at[chip, core], 2, c_sem.at[C_SIB], sibling)

    for h in range(heads):
        cols = slice(h * DH, (h + 1) * DH)
        dmix = dmixed[h]
        back = jnp.where(causal, dot(dmix, v[:, cols], (1, 1)), 0.0).astype(BF16)
        grad_q = dot(back, k[:, cols], (1, 0)) + dot(dmix, prior[h * 8 : h * 8 + 8].reshape(DH, DH), (1, 1))
        gq_v[:, cols] = grad_q.astype(BF16)
        gk_part[h] = dot(back, q[:, cols], (0, 0))
        gv_part[h] = dot(attend[h], dmix, (0, 0))
    stores = [pltpu.make_async_copy(gq_v, gq_hbm, store_sem.at[0])]
    stores[0].start()

    mine = [(h // 2 + pairs) % pairs for h in [y - core + 8, y - core + 10, y - core + 6, y - core + 12]]
    for i in mine:
        arrived(nall.at[i, x_left * 2], n_sem.at[N_LEFT0, i])
        send(nall.at[i, x_left * 2], 5, n_sem.at[N_OPP0, 0], right)
        arrived(nall.at[i, x_right * 2 + 1], n_sem.at[N_RIGHT1, i])
        send(nall.at[i, x_right * 2 + 1], 5, n_sem.at[N_OPP1, 0], left)

    for d in range(dps):
        out_v[:, d * DH : (d + 1) * DH] = dot(normed[...], wall[d], (1, 1)).astype(BF16)
    stores.append(pltpu.make_async_copy(out_v, out_hbm, store_sem.at[1]))
    stores[1].start()

    arrived(b_recv.at[pl.ds(0, seqs - 1)], b_sem)

    def backward_sum(i, total):
        s = seqs - 1 - i
        l_send[s] = total.astype(BF16)
        return total + b_recv[s].astype(F32)

    lax.fori_loop(0, seqs, backward_sum, jnp.zeros((16, DH), F32), unroll=8)
    later[me] = l_send[me]
    exchange(l_send, later, 6, l_sem.at[y])

    arrived_columns(nx, c_sem.at[C_SIB])
    for chip in range(nx):
        for at in range(2):
            tokens = slice((2 * chip + at) * block, (2 * chip + at + 1) * block)
            ccolt[0:DH, tokens] = ccol[chip, at, :, 0:DH].T
            ccolt[DH:wide, tokens] = ccol[chip, at, :, DH:wide].T

    def arrived_heads(sem):
        arrived(nall.at[0, pl.ds(0, pairs)], sem)

    for i in range(pairs):
        arrived(nall.at[i, x_left * 2 + 1], n_sem.at[N_LEFT1, i])
        arrived(nall.at[i, x_right * 2], n_sem.at[N_RIGHT0, i])
    arrived_heads(n_sem.at[N_SIB, 0])
    arrived_heads(n_sem.at[N_OPP0, 0])
    arrived_heads(n_sem.at[N_OPP1, 0])

    factor = 1.0 / math.sqrt(dps * block * seqs)
    for i in range(pairs):
        g_tile[i] = dot(ccolt[...], nall[i].reshape(dps * block, DH), (1, 0)) * factor
        for at in range(2):
            for r in range(2):
                rows = g_tile[i, pl.ds(at * DH + r, seqs, stride=2), :]
                g_rows[pl.ds(4 * i + 2 * at + r, seqs, stride=16), :] = rows

    for s in range(seqs):
        g_send[s] = g_rows[s * 16 : s * 16 + 16, :].astype(BF16)
    g_recv[me] = g_send[me]
    exchange(g_send, g_recv, 7, g_sem)

    arrived(later.at[pl.ds(0, nz - 1)], l_sem.at[y])
    for h in near_rows:
        arrived(later.at[pl.ds(h * 8, 8)], l_sem.at[h])
    for h in range(heads):
        cols = slice(h * DH, (h + 1) * DH)
        state = later[h * 8 : h * 8 + 8].reshape(DH, DH)
        gk_v[:, cols] = (gk_part[h] + dot(v[:, cols], state, (1, 1))).astype(BF16)
        gv_v[:, cols] = (gv_part[h] + dot(k[:, cols], state, (1, 0))).astype(BF16)
    stores.append(pltpu.make_async_copy(gk_v, gk_hbm, store_sem.at[2]))
    stores.append(pltpu.make_async_copy(gv_v, gv_hbm, store_sem.at[3]))
    stores[2].start()
    stores[3].start()

    def sent(ref, i):
        remote(ref, ref, send_sem.at[i], a_sem, sibling, me).wait_send()

    sent(wall.at[pl.ds(0, 7)], 0)
    sent(a_send.at[pl.ds(0, seqs - 1)], 1)
    sent(ccol.at[pl.ds(0, nx - 1), 0], 2)
    sent(ccol.at[pl.ds(0, nx), 0], 2)
    sent(p_send.at[pl.ds(0, seqs - 1)], 3)
    sent(b_send.at[pl.ds(0, seqs - 1)], 4)
    sent(nall.at[pl.ds(0, 3)], 5)
    sent(nall.at[0, pl.ds(0, 4)], 5)
    sent(l_send.at[pl.ds(0, seqs - 1)], 6)

    arrived(g_recv.at[pl.ds(0, seqs - 1)], g_sem)
    total = lax.fori_loop(0, seqs, lambda s, t: t + g_recv[s].astype(F32), jnp.zeros((16, DH), F32), unroll=8)
    g_sum[...] = total
    swap = remote(g_sum, g_other, send_sem.at[8], swap_sem, sibling, me)
    swap.start()
    swap.wait()
    theirs = g_other[...]
    even = jnp.where(core == 0, total, theirs)
    odd = jnp.where(core == 0, theirs, total)
    for h in range(heads):
        source = even if h % 2 == 0 else odd
        at = 4 * (h // 2)
        gw_v[:, h * DH : (h + 1) * DH] = jnp.where(core == 0, source[at : at + 2], source[at + 2 : at + 4])
    stores.append(pltpu.make_async_copy(gw_v, gw_hbm, store_sem.at[4]))
    stores[4].start()
    sent(g_send.at[pl.ds(0, seqs - 1)], 7)
    for store in stores:
        store.wait()


def place(*refs):
    count = len(refs) // 2
    sems = refs[-1]
    copies = [pltpu.make_async_copy(refs[i], refs[count + i], sems.at[i]) for i in range(count)]
    for copy in copies:
        copy.start()
    for copy in copies:
        copy.wait()


def local(sizes, queries, keys, values, cotangent, out_weight):
    dps, ny, nz, heads = sizes
    _, block, features = queries.shape
    seqs = ny * nz
    shapes = [jax.ShapeDtypeStruct((block, features), BF16)] * 4 + [jax.ShapeDtypeStruct((2, features), F32)]
    arguments = (queries[0], keys[0], values[0], cotangent[0], out_weight)
    states = pltpu.VMEM((seqs, 16, DH), BF16)
    whole = pltpu.VMEM((block, features), BF16)
    per_head = pltpu.VMEM((heads, block, DH), F32)
    dma = pltpu.SemaphoreType.DMA
    piece = pltpu.VMEM((16, DH), F32)
    out = pl.pallas_call(
        functools.partial(kernel, sizes),
        out_shape=shapes,
        in_specs=[pl.BlockSpec(memory_space=pl.ANY)] * 5,
        out_specs=[pl.BlockSpec(memory_space=pl.ANY)] * 5,
        scratch_shapes=[
            whole, whole, whole, whole,
            pltpu.VMEM((dps, block, features), BF16),
            pltpu.VMEM((block, features), F32),
            states, states, states, states,
            states, states, states, states,
            pltpu.VMEM((heads, block, block), BF16),
            per_head,
            whole,
            pltpu.VMEM((heads, block, DH), BF16),
            pltpu.VMEM((heads, block, DH), BF16),
            pltpu.VMEM((heads // 2, dps, block, DH), BF16),
            pltpu.VMEM((dps // 2, 2, block, 2 * DH), BF16),
            pltpu.VMEM((2 * DH, dps * block), BF16),
            per_head, per_head,
            pltpu.VMEM((heads // 2, 2 * DH, DH), F32),
            pltpu.VMEM((seqs * 16, DH), F32),
            states, states, piece, piece,
            whole, whole, whole, whole,
            pltpu.VMEM((2, features), F32),
            dma((5,)), dma((5,)), dma((9,)), dma, dma((heads,)), dma, dma((heads,)), dma,
            dma((10,)), dma((2,)), dma((7, heads // 2)), dma,
        ],
        compiler_params=pltpu.CompilerParams(
            collective_id=0, has_side_effects=True, vmem_limit_bytes=VMEM_LIMIT
        ),
        name="layer",
    )(*(pltpu.with_memory_space_constraint(a, pltpu.HBM) for a in arguments))
    out = pl.pallas_call(
        place,
        out_shape=shapes,
        in_specs=[pl.BlockSpec(memory_space=pl.ANY)] * 5,
        out_specs=[pl.BlockSpec(memory_space=pl.ANY)] * 5,
        scratch_shapes=[dma((5,))],
        compiler_params=pltpu.CompilerParams(vmem_limit_bytes=VMEM_LIMIT),
        name="place",
    )(*out)
    return tuple(part[None] for part in out[:4]) + (out[4],)


def solution(mesh):
    seqs = mesh.shape["seq"]
    ny = nz = math.isqrt(seqs)
    sizes = (mesh.shape["dp"], ny, nz, 8)
    tokens = P("dp", "seq", None)
    return jax.shard_map(
        functools.partial(local, sizes),
        mesh=mesh,
        in_specs=(tokens, tokens, tokens, tokens, P("dp", None)),
        out_specs=(tokens, tokens, tokens, tokens, P(("dp", "seq"), None)),
        check_vma=False,
    )
```

```python
import functools
import math

import jax
import jax.numpy as jnp
from jax import lax
from jax.experimental import pallas as pl
from jax.experimental.pallas import tpu as pltpu
from jax.sharding import PartitionSpec as P

MESH = pl.DeviceIdType.MESH
DH = 128
EPSILON = 1e-05
BF16 = jnp.bfloat16
F32 = jnp.float32
VMEM_LIMIT = 40 * 1024 * 1024


def dot(left, right, contract):
    return lax.dot_general(left, right, ((contract[:1], contract[1:]), ((), ())), preferred_element_type=F32)


def head_cols(h):
    return pl.ds(pl.multiple_of(h * DH, DH), DH)


def apart(offset, count):
    return min(offset, count - offset)


def far_first(ny, nz):
    offsets = [(dy, dz) for dy in range(ny) for dz in range(nz)]
    return sorted(offsets, key=lambda o: -(apart(o[0], ny) + apart(o[1], nz)))


def kernel(
    sizes,
    q_hbm, k_hbm, v_hbm, c_hbm, w_hbm,
    out_hbm, gq_hbm, gk_hbm, gv_hbm, gw_hbm,
    q, k, v, c, wall, dn,
    a_send, a_recv, p_send, prior,
    b_send, b_recv, l_send, later,
    attend, part, normed, dmixed, n_send, nall, ccolt,
    gk_part, gv_part, g_tile, g_rows, g_send, g_recv, g_out, g_in,
    out_v, gq_v, gk_v, gv_v, gw_v,
    load_sem, store_sem, send_sem, a_sem, p_sem, b_sem, l_sem, g_sem,
    w_sem, c_sem, n_sem, swap_sem,
):
    dps, ny, nz, heads = sizes
    nx = dps // 2
    seqs = ny * nz
    block = q.shape[0]
    half = block // 2
    me_dp, me = lax.axis_index("dp"), lax.axis_index("seq")
    x, core = me_dp // 2, me_dp % 2
    y, z = me // nz, me % nz
    x_right, x_left, x_opposite = (x + 1) % nx, (x + nx - 1) % nx, (x + 2) % nx
    other = 1 - core
    right, left, opposite = x_right * 2 + core, x_left * 2 + core, x_opposite * 2 + core
    sibling = x * 2 + other
    right_s, left_s, opposite_s = x_right * 2 + other, x_left * 2 + other, x_opposite * 2 + other

    rows = [(y + d) % ny for d in range(ny)]
    columns = [(z + d) % nz for d in range(nz)]
    others = far_first(ny, nz)[:-1]
    mine = z * ny + y
    near_columns = sorted(range(nz), key=lambda d: apart(d, nz))
    halves = (near_columns[: nz // 2], near_columns[nz // 2 :])

    loads = [
        pltpu.make_async_copy(src, dst, load_sem.at[i])
        for i, (src, dst) in enumerate(
            [(k_hbm, k), (v_hbm, v), (w_hbm, wall.at[me_dp]), (q_hbm, q), (c_hbm, c)]
        )
    ]
    for load in loads:
        load.start()

    barrier = pltpu.get_barrier_semaphore()

    def greet(dp, seq):
        pl.semaphore_signal(barrier, inc=1, device_id=(dp, seq), device_id_type=MESH)

    for dy, dz in others:
        greet(me_dp, rows[dy] * nz + columns[dz])
    for dp in (opposite, opposite_s, right, left, right_s, left_s, sibling):
        greet(dp, me)

    loads[0].wait()
    loads[1].wait()
    for h in range(heads):
        cols = slice(h * DH, (h + 1) * DH)
        a_send[h * 8 : h * 8 + 8] = dot(k[:, cols], v[:, cols], (0, 0)).astype(BF16).reshape(8, 16, DH)
    a_recv[me] = a_send[mine]
    loads[2].wait()
    pl.semaphore_wait(barrier, seqs - 1 + dps - 1)

    def remote(src, dst, send, recv, dp, seq):
        return pltpu.make_async_remote_copy(
            src_ref=src, dst_ref=dst, send_sem=send, recv_sem=recv, device_id=(dp, seq), device_id_type=MESH
        )

    def send(ref, group, recv, dp):
        remote(ref, ref, send_sem.at[group], recv, dp, me).start()

    def arrived(ref, sem):
        remote(ref, ref, send_sem.at[0], sem, sibling, me).wait_recv()

    def to_owners(source, landing, group, recv, offsets):
        for dy, dz in offsets:
            row, column = rows[dy], columns[dz]
            piece = source.at[column * ny + row]
            remote(piece, landing.at[me], send_sem.at[group], recv, me_dp, row * nz + column).start()

    def give_back(source, landing, slot, group, recv):
        for dy, dz in others:
            seq = rows[dy] * nz + columns[dz]
            remote(source.at[seq], landing.at[slot], send_sem.at[group], recv, me_dp, seq).start()

    def given_back(landing, dz, recv):
        count = ny - 1 if dz == 0 else ny
        arrived(landing.at[pl.ds(0, count)], recv.at[columns[dz]])

    W_LEFT0, W_LEFT1, W_RIGHT0, W_RIGHT1, W_OPP0, W_OPP1, W_SIB, W_SIB_LEFT, W_SIB_RIGHT, W_SIB_OPP = range(10)
    low, high = pl.ds(0, half), pl.ds(half, half)
    send(wall.at[me_dp, low], 0, w_sem.at[W_LEFT0], right)
    send(wall.at[me_dp, high], 0, w_sem.at[W_RIGHT1], left)
    to_owners(a_send, a_recv, 1, a_sem, others)
    send(wall.at[me_dp, high], 0, w_sem.at[W_LEFT1], right)
    send(wall.at[me_dp, low], 0, w_sem.at[W_RIGHT0], left)
    send(wall.at[me_dp], 0, w_sem.at[W_SIB], sibling)

    loads[3].wait()
    causal = lax.broadcasted_iota(jnp.int32, (block, block), 0) >= lax.broadcasted_iota(
        jnp.int32, (block, block), 1
    )
    for h in range(heads):
        cols = slice(h * DH, (h + 1) * DH)
        near = jnp.where(causal, dot(q[:, cols], k[:, cols], (1, 1)), 0.0).astype(BF16)
        attend[h] = near
        part[h] = dot(near, v[:, cols], (1, 0))

    arrived(wall.at[left, low], w_sem.at[W_LEFT0])
    send(wall.at[left, low], 0, w_sem.at[W_OPP0], right)
    arrived(wall.at[right, high], w_sem.at[W_RIGHT1])
    send(wall.at[right, high], 0, w_sem.at[W_OPP1], left)

    loads[4].wait()
    own_c = ccolt.at[:, head_cols(me_dp)]
    for h in range(heads):
        rows_h = slice(h * DH, (h + 1) * DH)
        ccolt[rows_h, head_cols(me_dp)] = c[:, rows_h].T
    C_LEFT, C_RIGHT, C_OPP, C_SIB, C_SIB_LEFT, C_SIB_RIGHT, C_SIB_OPP = range(7)
    send(own_c, 2, c_sem.at[C_LEFT], right)
    send(own_c, 2, c_sem.at[C_RIGHT], left)
    send(own_c, 2, c_sem.at[C_OPP], opposite)
    send(own_c, 2, c_sem.at[C_SIB], sibling)

    arrived(a_recv.at[pl.ds(0, seqs - 1)], a_sem)

    def forward_sum(s, total):
        p_send[s] = total.astype(BF16)
        return total + a_recv[s].astype(F32)

    lax.fori_loop(0, seqs, forward_sum, jnp.zeros((16, DH), F32), unroll=8)
    prior[mine] = p_send[me]
    give_back(p_send, prior, mine, 3, p_sem.at[z])

    arrived(wall.at[left, high], w_sem.at[W_LEFT1])
    send(wall.at[left], 0, w_sem.at[W_SIB_LEFT], sibling)
    arrived(wall.at[right, low], w_sem.at[W_RIGHT0])
    send(wall.at[right], 0, w_sem.at[W_SIB_RIGHT], sibling)
    arrived(wall.at[opposite, low], w_sem.at[W_OPP0])
    arrived(wall.at[opposite, high], w_sem.at[W_OPP1])
    send(wall.at[opposite], 0, w_sem.at[W_SIB_OPP], sibling)

    arrived(wall.at[sibling], w_sem.at[W_SIB])
    arrived(wall.at[left_s], w_sem.at[W_SIB_LEFT])
    arrived(wall.at[right_s], w_sem.at[W_SIB_RIGHT])
    arrived(wall.at[opposite_s], w_sem.at[W_SIB_OPP])
    dn[...] = dot(c[...], wall[...].reshape(dps * block, heads * DH), (1, 0))

    for half_dz in halves:
        group = [columns[dz] for dz in half_dz]
        for dz in half_dz:
            given_back(prior, dz, p_sem)
        kept = []
        for h in group:
            mixed = part[h] + dot(q[:, head_cols(h)], prior[pl.ds(h * 8, 8)].reshape(DH, DH), (1, 0))
            inverse = lax.rsqrt(jnp.mean(mixed * mixed, axis=-1, keepdims=True) + EPSILON)
            n = mixed * inverse
            n_send[h] = n.astype(BF16)
            kept.append((n, inverse))
        for h in group:
            @pl.when(h != me_dp)
            def _(h=h):
                remote(n_send.at[h], nall.at[me_dp], send_sem.at[5], n_sem, h, me).start()

        for h, (n, inverse) in zip(group, kept):
            dnormed = dn[:, head_cols(h)]
            dmix = (dnormed - n * jnp.mean(dnormed * n, axis=-1, keepdims=True)) * inverse
            dmix = dmix.astype(BF16)
            u = dot(q[:, head_cols(h)], dmix, (0, 0))
            b_send[pl.ds(h * 8, 8)] = u.astype(BF16).reshape(8, 16, DH)
            dmixed[h] = dmix
            normed[:, head_cols(h)] = n.astype(BF16)
        to_owners(b_send, b_recv, 4, b_sem, [o for o in others if o[1] in half_dz])
    b_recv[me] = b_send[mine]
    nall[me_dp] = n_send[me_dp]

    for dp, here, there in ((left, C_LEFT, C_SIB_LEFT), (right, C_RIGHT, C_SIB_RIGHT), (opposite, C_OPP, C_SIB_OPP)):
        tokens = ccolt.at[:, head_cols(dp)]
        arrived(tokens, c_sem.at[here])
        send(tokens, 2, c_sem.at[there], sibling)

    for dp, there in ((sibling, C_SIB), (left_s, C_SIB_LEFT), (right_s, C_SIB_RIGHT), (opposite_s, C_SIB_OPP)):
        arrived(ccolt.at[:, head_cols(dp)], c_sem.at[there])
    arrived(nall.at[pl.ds(0, dps - 1)], n_sem)
    factor = 1.0 / math.sqrt(dps * block * seqs)
    g_tile[...] = dot(ccolt[...], nall[...].reshape(dps * block, DH), (1, 0)) * factor
    for d in range(dps):
        for r in range(2):
            g_rows[pl.ds(2 * d + r, seqs, stride=16), :] = g_tile[pl.ds(d * block + r, seqs, stride=2), :]
    for s in range(seqs):
        g_send[s] = g_rows[s * 16 : s * 16 + 16, :].astype(BF16)
    g_recv[me] = g_send[me]

    def sum_back():
        arrived(b_recv.at[pl.ds(0, seqs - 1)], b_sem)

        def backward_sum(i, total):
            s = seqs - 1 - i
            l_send[s] = total.astype(BF16)
            return total + b_recv[s].astype(F32)

        lax.fori_loop(0, seqs, backward_sum, jnp.zeros((16, DH), F32), unroll=8)
        later[mine] = l_send[me]
        give_back(l_send, later, mine, 6, l_sem.at[z])

    give_back(g_send, g_recv, me, 7, g_sem)
    sum_back()

    for h in range(heads):
        cols = slice(h * DH, (h + 1) * DH)
        dmix = dmixed[h]
        back = jnp.where(causal, dot(dmix, v[:, cols], (1, 1)), 0.0).astype(BF16)
        grad_q = dot(back, k[:, cols], (1, 0)) + dot(dmix, prior[h * 8 : h * 8 + 8].reshape(DH, DH), (1, 1))
        gq_v[:, cols] = grad_q.astype(BF16)
        gk_part[h] = dot(back, q[:, cols], (0, 0))
        gv_part[h] = dot(attend[h], dmix, (0, 0))
    stores = [pltpu.make_async_copy(gq_v, gq_hbm, store_sem.at[0])]
    stores[0].start()

    for d in range(dps):
        out_v[:, d * DH : (d + 1) * DH] = dot(normed[...], wall[d], (1, 1)).astype(BF16)
    stores.append(pltpu.make_async_copy(out_v, out_hbm, store_sem.at[1]))
    stores[1].start()

    arrived(g_recv.at[pl.ds(0, seqs - 1)], g_sem)
    total = lax.fori_loop(0, seqs, lambda s, t: t + g_recv[s].astype(F32), jnp.zeros((16, DH), F32), unroll=8)
    for d in range(dps):
        g_out[d] = total[2 * d : 2 * d + 2]
    g_in[me_dp] = g_out[me_dp]
    for dp in (opposite, opposite_s, right, right_s, left, left_s, sibling):
        remote(g_out.at[dp], g_in.at[me_dp], send_sem.at[8], swap_sem, dp, me).start()

    for half_dz in halves:
        for dz in half_dz:
            given_back(later, dz, l_sem)
        for dz in half_dz:
            h = columns[dz]
            cols = head_cols(h)
            state = later[pl.ds(h * 8, 8)].reshape(DH, DH)
            gk_v[:, cols] = (gk_part[h] + dot(v[:, cols], state, (1, 1))).astype(BF16)
            gv_v[:, cols] = (gv_part[h] + dot(k[:, cols], state, (1, 0))).astype(BF16)
    stores.append(pltpu.make_async_copy(gk_v, gk_hbm, store_sem.at[2]))
    stores.append(pltpu.make_async_copy(gv_v, gv_hbm, store_sem.at[3]))
    stores[2].start()
    stores[3].start()

    def sent(ref, i):
        remote(ref, ref, send_sem.at[i], a_sem, sibling, me).wait_send()

    sent(wall.at[pl.ds(0, 7)], 0)
    sent(a_send.at[pl.ds(0, seqs - 1)], 1)
    sent(ccolt.at[:, pl.ds(0, 7 * block)], 2)
    sent(p_send.at[pl.ds(0, seqs - 1)], 3)
    sent(b_send.at[pl.ds(0, seqs - 1)], 4)
    sent(nall.at[pl.ds(0, dps - 1)], 5)
    sent(l_send.at[pl.ds(0, seqs - 1)], 6)

    sent(g_send.at[pl.ds(0, seqs - 1)], 7)
    sent(g_out.at[pl.ds(0, dps - 1)], 8)
    arrived(g_in.at[pl.ds(0, dps - 1)], swap_sem)
    for d in range(dps):
        gw_v[:, d * DH : (d + 1) * DH] = g_in[d]
    stores.append(pltpu.make_async_copy(gw_v, gw_hbm, store_sem.at[4]))
    stores[4].start()
    for store in stores:
        store.wait()


def place(*refs):
    count = len(refs) // 2
    sems = refs[-1]
    copies = [pltpu.make_async_copy(refs[i], refs[count + i], sems.at[i]) for i in range(count)]
    for copy in copies:
        copy.start()
    for copy in copies:
        copy.wait()


def local(sizes, queries, keys, values, cotangent, out_weight):
    dps, ny, nz, heads = sizes
    _, block, features = queries.shape
    seqs = ny * nz
    shapes = [jax.ShapeDtypeStruct((block, features), BF16)] * 4 + [jax.ShapeDtypeStruct((2, features), F32)]
    arguments = (queries[0], keys[0], values[0], cotangent[0], out_weight)
    states = pltpu.VMEM((seqs, 16, DH), BF16)
    whole = pltpu.VMEM((block, features), BF16)
    per_head = pltpu.VMEM((heads, block, DH), F32)
    dma = pltpu.SemaphoreType.DMA
    piece = pltpu.VMEM((dps, 2, DH), F32)
    out = pl.pallas_call(
        functools.partial(kernel, sizes),
        out_shape=shapes,
        in_specs=[pl.BlockSpec(memory_space=pl.ANY)] * 5,
        out_specs=[pl.BlockSpec(memory_space=pl.ANY)] * 5,
        scratch_shapes=[
            whole, whole, whole, whole,
            pltpu.VMEM((dps, block, features), BF16),
            pltpu.VMEM((block, features), F32),
            states, states, states, states,
            states, states, states, states,
            pltpu.VMEM((heads, block, block), BF16),
            per_head,
            whole,
            pltpu.VMEM((heads, block, DH), BF16),
            pltpu.VMEM((heads, block, DH), BF16),
            pltpu.VMEM((dps, block, DH), BF16),
            pltpu.VMEM((features, dps * block), BF16),
            per_head, per_head,
            pltpu.VMEM((features, DH), F32),
            pltpu.VMEM((seqs * 16, DH), F32),
            states, states, piece, piece,
            whole, whole, whole, whole,
            pltpu.VMEM((2, features), F32),
            dma((5,)), dma((5,)), dma((9,)), dma, dma((heads,)), dma, dma((heads,)), dma,
            dma((10,)), dma((7,)), dma, dma,
        ],
        compiler_params=pltpu.CompilerParams(
            collective_id=0, has_side_effects=True, vmem_limit_bytes=VMEM_LIMIT
        ),
        name="layer",
    )(*(pltpu.with_memory_space_constraint(a, pltpu.HBM) for a in arguments))
    out = pl.pallas_call(
        place,
        out_shape=shapes,
        in_specs=[pl.BlockSpec(memory_space=pl.ANY)] * 5,
        out_specs=[pl.BlockSpec(memory_space=pl.ANY)] * 5,
        scratch_shapes=[dma((5,))],
        compiler_params=pltpu.CompilerParams(vmem_limit_bytes=VMEM_LIMIT),
        name="place",
    )(*out)
    return tuple(part[None] for part in out[:4]) + (out[4],)


def solution(mesh):
    seqs = mesh.shape["seq"]
    ny = nz = math.isqrt(seqs)
    sizes = (mesh.shape["dp"], ny, nz, 8)
    tokens = P("dp", "seq", None)
    return jax.shard_map(
        functools.partial(local, sizes),
        mesh=mesh,
        in_specs=(tokens, tokens, tokens, tokens, P("dp", None)),
        out_specs=(tokens, tokens, tokens, tokens, P(("dp", "seq"), None)),
        check_vma=False,
    )
```

```python
import functools
import math

import jax
import jax.numpy as jnp
from jax import lax
from jax.experimental import pallas as pl
from jax.experimental.pallas import tpu as pltpu
from jax.sharding import PartitionSpec as P

MESH = pl.DeviceIdType.MESH
DH = 128
EPSILON = 1e-05
BF16 = jnp.bfloat16
F32 = jnp.float32
VMEM_LIMIT = 40 * 1024 * 1024


def dot(left, right, contract):
    return lax.dot_general(left, right, ((contract[:1], contract[1:]), ((), ())), preferred_element_type=F32)


def head_cols(h):
    return pl.ds(pl.multiple_of(h * DH, DH), DH)


def apart(offset, count):
    return min(offset, count - offset)


def far_first(ny, nz):
    offsets = [(dy, dz) for dy in range(ny) for dz in range(nz)]
    return sorted(offsets, key=lambda o: -(apart(o[0], ny) + apart(o[1], nz)))


def kernel(
    sizes,
    q_hbm, k_hbm, v_hbm, c_hbm, w_hbm,
    out_v, gq_v, gk_v, gv_v, gw_v,
    q, k, v, c, wall, dn,
    a_send, a_recv, p_send, prior,
    b_send, b_recv, l_send, later,
    attend, part, normed, dmixed, n_send, nall, ccolt,
    gk_part, gv_part, g_tile, g_rows, g_send, g_recv, g_out, g_in,
    load_sem, send_sem, a_sem, p_sem, b_sem, l_sem, g_sem,
    w_sem, c_sem, n_sem, swap_sem,
):
    dps, ny, nz, heads = sizes
    nx = dps // 2
    seqs = ny * nz
    block = q.shape[0]
    half = block // 2
    me_dp, me = lax.axis_index("dp"), lax.axis_index("seq")
    x, core = me_dp // 2, me_dp % 2
    y, z = me // nz, me % nz
    x_right, x_left, x_opposite = (x + 1) % nx, (x + nx - 1) % nx, (x + 2) % nx
    other = 1 - core
    right, left, opposite = x_right * 2 + core, x_left * 2 + core, x_opposite * 2 + core
    sibling = x * 2 + other
    right_s, left_s, opposite_s = x_right * 2 + other, x_left * 2 + other, x_opposite * 2 + other

    rows = [(y + d) % ny for d in range(ny)]
    columns = [(z + d) % nz for d in range(nz)]
    others = far_first(ny, nz)[:-1]
    mine = z * ny + y
    near_columns = sorted(range(nz), key=lambda d: apart(d, nz))
    halves = (near_columns[: nz // 2], near_columns[nz // 2 :])

    loads = [
        pltpu.make_async_copy(src, dst, load_sem.at[i])
        for i, (src, dst) in enumerate(
            [(k_hbm, k), (v_hbm, v), (w_hbm, wall.at[me_dp]), (q_hbm, q), (c_hbm, c)]
        )
    ]
    for load in loads:
        load.start()

    barrier = pltpu.get_barrier_semaphore()

    def greet(dp, seq):
        pl.semaphore_signal(barrier, inc=1, device_id=(dp, seq), device_id_type=MESH)

    for dy, dz in others:
        greet(me_dp, rows[dy] * nz + columns[dz])
    for dp in (opposite, opposite_s, right, left, right_s, left_s, sibling):
        greet(dp, me)

    loads[0].wait()
    loads[1].wait()
    for h in range(heads):
        cols = slice(h * DH, (h + 1) * DH)
        a_send[h * 8 : h * 8 + 8] = dot(k[:, cols], v[:, cols], (0, 0)).astype(BF16).reshape(8, 16, DH)
    a_recv[me] = a_send[mine]
    loads[2].wait()
    pl.semaphore_wait(barrier, seqs - 1 + dps - 1)

    def remote(src, dst, send, recv, dp, seq):
        return pltpu.make_async_remote_copy(
            src_ref=src, dst_ref=dst, send_sem=send, recv_sem=recv, device_id=(dp, seq), device_id_type=MESH
        )

    def send(ref, group, recv, dp):
        remote(ref, ref, send_sem.at[group], recv, dp, me).start()

    def arrived(ref, sem):
        remote(ref, ref, send_sem.at[0], sem, sibling, me).wait_recv()

    def to_owners(source, landing, group, recv, offsets):
        for dy, dz in offsets:
            row, column = rows[dy], columns[dz]
            piece = source.at[column * ny + row]
            remote(piece, landing.at[me], send_sem.at[group], recv, me_dp, row * nz + column).start()

    def give_back(source, landing, slot, group, recv):
        for dy, dz in others:
            seq = rows[dy] * nz + columns[dz]
            remote(source.at[seq], landing.at[slot], send_sem.at[group], recv, me_dp, seq).start()

    def given_back(landing, dz, recv):
        count = ny - 1 if dz == 0 else ny
        arrived(landing.at[pl.ds(0, count)], recv.at[columns[dz]])

    W_LEFT0, W_LEFT1, W_RIGHT0, W_RIGHT1, W_OPP0, W_OPP1, W_SIB, W_SIB_LEFT, W_SIB_RIGHT, W_SIB_OPP = range(10)
    low, high = pl.ds(0, half), pl.ds(half, half)
    send(wall.at[me_dp, low], 0, w_sem.at[W_LEFT0], right)
    send(wall.at[me_dp, high], 0, w_sem.at[W_RIGHT1], left)
    to_owners(a_send, a_recv, 1, a_sem, others)
    send(wall.at[me_dp, high], 0, w_sem.at[W_LEFT1], right)
    send(wall.at[me_dp, low], 0, w_sem.at[W_RIGHT0], left)
    send(wall.at[me_dp], 0, w_sem.at[W_SIB], sibling)

    loads[3].wait()
    causal = lax.broadcasted_iota(jnp.int32, (block, block), 0) >= lax.broadcasted_iota(
        jnp.int32, (block, block), 1
    )
    for h in range(heads):
        cols = slice(h * DH, (h + 1) * DH)
        near = jnp.where(causal, dot(q[:, cols], k[:, cols], (1, 1)), 0.0).astype(BF16)
        attend[h] = near
        part[h] = dot(near, v[:, cols], (1, 0))

    arrived(wall.at[left, low], w_sem.at[W_LEFT0])
    send(wall.at[left, low], 0, w_sem.at[W_OPP0], right)
    arrived(wall.at[right, high], w_sem.at[W_RIGHT1])
    send(wall.at[right, high], 0, w_sem.at[W_OPP1], left)

    loads[4].wait()
    own_c = ccolt.at[:, head_cols(me_dp)]
    for h in range(heads):
        rows_h = slice(h * DH, (h + 1) * DH)
        g_tile[rows_h, :] = c[:, rows_h].astype(F32).T
        for r in range(2):
            g_rows[pl.ds(2 * h + r, seqs, stride=16), :] = g_tile[pl.ds(h * DH + r, seqs, stride=2), :]
    ccolt[:, head_cols(me_dp)] = g_rows[...].astype(BF16)
    C_LEFT, C_RIGHT, C_OPP, C_SIB, C_SIB_LEFT, C_SIB_RIGHT, C_SIB_OPP = range(7)
    send(own_c, 2, c_sem.at[C_LEFT], right)
    send(own_c, 2, c_sem.at[C_RIGHT], left)
    send(own_c, 2, c_sem.at[C_OPP], opposite)
    send(own_c, 2, c_sem.at[C_SIB], sibling)

    arrived(a_recv.at[pl.ds(0, seqs - 1)], a_sem)

    def forward_sum(s, total):
        p_send[s] = total.astype(BF16)
        return total + a_recv[s].astype(F32)

    lax.fori_loop(0, seqs, forward_sum, jnp.zeros((16, DH), F32), unroll=8)
    prior[mine] = p_send[me]
    give_back(p_send, prior, mine, 3, p_sem.at[z])

    arrived(wall.at[left, high], w_sem.at[W_LEFT1])
    send(wall.at[left], 0, w_sem.at[W_SIB_LEFT], sibling)
    arrived(wall.at[right, low], w_sem.at[W_RIGHT0])
    send(wall.at[right], 0, w_sem.at[W_SIB_RIGHT], sibling)
    arrived(wall.at[opposite, low], w_sem.at[W_OPP0])
    arrived(wall.at[opposite, high], w_sem.at[W_OPP1])
    send(wall.at[opposite], 0, w_sem.at[W_SIB_OPP], sibling)

    arrived(wall.at[sibling], w_sem.at[W_SIB])
    arrived(wall.at[left_s], w_sem.at[W_SIB_LEFT])
    arrived(wall.at[right_s], w_sem.at[W_SIB_RIGHT])
    arrived(wall.at[opposite_s], w_sem.at[W_SIB_OPP])
    dn[...] = dot(c[...], wall[...].reshape(dps * block, heads * DH), (1, 0))

    for half_dz in halves:
        group = [columns[dz] for dz in half_dz]
        for dz in half_dz:
            given_back(prior, dz, p_sem)
        kept = []
        for h in group:
            mixed = part[h] + dot(q[:, head_cols(h)], prior[pl.ds(h * 8, 8)].reshape(DH, DH), (1, 0))
            inverse = lax.rsqrt(jnp.mean(mixed * mixed, axis=-1, keepdims=True) + EPSILON)
            n = mixed * inverse
            n_send[h] = n.astype(BF16)
            kept.append((n, inverse))
        for h, (n, inverse) in zip(group, kept):
            dnormed = dn[:, head_cols(h)]
            dmix = (dnormed - n * jnp.mean(dnormed * n, axis=-1, keepdims=True)) * inverse
            dmix = dmix.astype(BF16)
            u = dot(q[:, head_cols(h)], dmix, (0, 0))
            b_send[pl.ds(h * 8, 8)] = u.astype(BF16).reshape(8, 16, DH)
            dmixed[h] = dmix
            normed[:, head_cols(h)] = n.astype(BF16)
        to_owners(b_send, b_recv, 4, b_sem, [o for o in others if o[1] in half_dz])
        for h in group:
            @pl.when(h != me_dp)
            def _(h=h):
                remote(n_send.at[h], nall.at[me_dp], send_sem.at[5], n_sem, h, me).start()

    b_recv[me] = b_send[mine]
    nall[me_dp] = n_send[me_dp]

    for dp, here, there in ((left, C_LEFT, C_SIB_LEFT), (right, C_RIGHT, C_SIB_RIGHT), (opposite, C_OPP, C_SIB_OPP)):
        tokens = ccolt.at[:, head_cols(dp)]
        arrived(tokens, c_sem.at[here])
        send(tokens, 2, c_sem.at[there], sibling)

    for dp, there in ((sibling, C_SIB), (left_s, C_SIB_LEFT), (right_s, C_SIB_RIGHT), (opposite_s, C_SIB_OPP)):
        arrived(ccolt.at[:, head_cols(dp)], c_sem.at[there])
    arrived(nall.at[pl.ds(0, dps - 1)], n_sem)
    factor = 1.0 / math.sqrt(dps * block * seqs)
    g = dot(ccolt[...], nall[...].reshape(dps * block, DH), (1, 0)) * factor
    g_send[...] = g.astype(BF16).reshape(seqs, 16, DH)
    g_recv[me] = g_send[me]

    def sum_back():
        arrived(b_recv.at[pl.ds(0, seqs - 1)], b_sem)

        def backward_sum(i, total):
            s = seqs - 1 - i
            l_send[s] = total.astype(BF16)
            return total + b_recv[s].astype(F32)

        lax.fori_loop(0, seqs, backward_sum, jnp.zeros((16, DH), F32), unroll=8)
        later[mine] = l_send[me]
        give_back(l_send, later, mine, 6, l_sem.at[z])

    give_back(g_send, g_recv, me, 7, g_sem)
    sum_back()

    for h in range(heads):
        cols = slice(h * DH, (h + 1) * DH)
        dmix = dmixed[h]
        back = jnp.where(causal, dot(dmix, v[:, cols], (1, 1)), 0.0).astype(BF16)
        grad_q = dot(back, k[:, cols], (1, 0)) + dot(dmix, prior[h * 8 : h * 8 + 8].reshape(DH, DH), (1, 1))
        gq_v[:, cols] = grad_q.astype(BF16)
        gk_part[h] = dot(back, q[:, cols], (0, 0))
        gv_part[h] = dot(attend[h], dmix, (0, 0))

    for d in range(dps):
        out_v[:, d * DH : (d + 1) * DH] = dot(normed[...], wall[d], (1, 1)).astype(BF16)

    arrived(g_recv.at[pl.ds(0, seqs - 1)], g_sem)
    total = lax.fori_loop(0, seqs, lambda s, t: t + g_recv[s].astype(F32), jnp.zeros((16, DH), F32), unroll=8)
    for d in range(dps):
        g_out[d] = total[2 * d : 2 * d + 2]
    g_in[me_dp] = g_out[me_dp]
    for dp in (opposite, opposite_s, right, right_s, left, left_s, sibling):
        remote(g_out.at[dp], g_in.at[me_dp], send_sem.at[8], swap_sem, dp, me).start()

    for half_dz in halves:
        for dz in half_dz:
            given_back(later, dz, l_sem)
        for dz in half_dz:
            h = columns[dz]
            cols = head_cols(h)
            state = later[pl.ds(h * 8, 8)].reshape(DH, DH)
            gk_v[:, cols] = (gk_part[h] + dot(v[:, cols], state, (1, 1))).astype(BF16)
            gv_v[:, cols] = (gv_part[h] + dot(k[:, cols], state, (1, 0))).astype(BF16)

    def sent(ref, i):
        remote(ref, ref, send_sem.at[i], a_sem, sibling, me).wait_send()

    sent(wall.at[pl.ds(0, 7)], 0)
    sent(a_send.at[pl.ds(0, seqs - 1)], 1)
    sent(ccolt.at[:, pl.ds(0, 7 * block)], 2)
    sent(p_send.at[pl.ds(0, seqs - 1)], 3)
    sent(b_send.at[pl.ds(0, seqs - 1)], 4)
    sent(nall.at[pl.ds(0, dps - 1)], 5)
    sent(l_send.at[pl.ds(0, seqs - 1)], 6)

    sent(g_send.at[pl.ds(0, seqs - 1)], 7)
    sent(g_out.at[pl.ds(0, dps - 1)], 8)
    arrived(g_in.at[pl.ds(0, dps - 1)], swap_sem)
    for d in range(dps):
        gw_v[:, d * DH : (d + 1) * DH] = g_in[d]


def place(*refs):
    count = len(refs) // 2
    sems = refs[-1]
    copies = [pltpu.make_async_copy(refs[i], refs[count + i], sems.at[i]) for i in range(count)]
    for copy in copies:
        copy.start()
    for copy in copies:
        copy.wait()


def local(sizes, queries, keys, values, cotangent, out_weight):
    dps, ny, nz, heads = sizes
    _, block, features = queries.shape
    seqs = ny * nz
    shapes = [jax.ShapeDtypeStruct((block, features), BF16)] * 4 + [jax.ShapeDtypeStruct((2, features), F32)]
    arguments = (queries[0], keys[0], values[0], cotangent[0], out_weight)
    states = pltpu.VMEM((seqs, 16, DH), BF16)
    whole = pltpu.VMEM((block, features), BF16)
    per_head = pltpu.VMEM((heads, block, DH), F32)
    dma = pltpu.SemaphoreType.DMA
    piece = pltpu.VMEM((dps, 2, DH), F32)
    out = pl.pallas_call(
        functools.partial(kernel, sizes),
        out_shape=[pltpu.VMEM(s.shape, s.dtype) for s in shapes],
        in_specs=[pl.BlockSpec(memory_space=pl.ANY)] * 5,
        out_specs=[pl.BlockSpec(memory_space=pltpu.VMEM)] * 5,
        scratch_shapes=[
            whole, whole, whole, whole,
            pltpu.VMEM((dps, block, features), BF16),
            pltpu.VMEM((block, features), F32),
            states, states, states, states,
            states, states, states, states,
            pltpu.VMEM((heads, block, block), BF16),
            per_head,
            whole,
            pltpu.VMEM((heads, block, DH), BF16),
            pltpu.VMEM((heads, block, DH), BF16),
            pltpu.VMEM((dps, block, DH), BF16),
            pltpu.VMEM((features, dps * block), BF16),
            per_head, per_head,
            pltpu.VMEM((features, DH), F32),
            pltpu.VMEM((seqs * 16, DH), F32),
            states, states, piece, piece,
            dma((5,)), dma((9,)), dma, dma((heads,)), dma, dma((heads,)), dma,
            dma((10,)), dma((7,)), dma, dma,
        ],
        compiler_params=pltpu.CompilerParams(
            collective_id=0, has_side_effects=True, vmem_limit_bytes=VMEM_LIMIT
        ),
        name="layer",
    )(*(pltpu.with_memory_space_constraint(a, pltpu.HBM) for a in arguments))
    out = pl.pallas_call(
        place,
        out_shape=shapes,
        in_specs=[pl.BlockSpec(memory_space=pl.ANY)] * 5,
        out_specs=[pl.BlockSpec(memory_space=pl.ANY)] * 5,
        scratch_shapes=[dma((5,))],
        compiler_params=pltpu.CompilerParams(vmem_limit_bytes=VMEM_LIMIT),
        name="place",
    )(*out)
    return tuple(part[None] for part in out[:4]) + (out[4],)


def solution(mesh):
    seqs = mesh.shape["seq"]
    ny = nz = math.isqrt(seqs)
    sizes = (mesh.shape["dp"], ny, nz, 8)
    tokens = P("dp", "seq", None)
    return jax.shard_map(
        functools.partial(local, sizes),
        mesh=mesh,
        in_specs=(tokens, tokens, tokens, tokens, P("dp", None)),
        out_specs=(tokens, tokens, tokens, tokens, P(("dp", "seq"), None)),
        check_vma=False,
    )
```

```python
import functools
import math

import jax
import jax.numpy as jnp
from jax import lax
from jax.experimental import pallas as pl
from jax.experimental.pallas import tpu as pltpu
from jax.sharding import PartitionSpec as P

MESH = pl.DeviceIdType.MESH
DH = 128
EPSILON = 1e-05
BF16 = jnp.bfloat16
F32 = jnp.float32
VMEM_LIMIT = 40 * 1024 * 1024


def dot(left, right, contract):
    return lax.dot_general(left, right, ((contract[:1], contract[1:]), ((), ())), preferred_element_type=F32)


def head_cols(h):
    return pl.ds(pl.multiple_of(h * DH, DH), DH)


def apart(offset, count):
    return min(offset, count - offset)


def far_first(ny, nz):
    offsets = [(dy, dz) for dy in range(ny) for dz in range(nz)]
    return sorted(offsets, key=lambda o: -(apart(o[0], ny) + apart(o[1], nz)))


def kernel(
    sizes,
    q_hbm, k_hbm, v_hbm, c_hbm, w_hbm,
    out_v, gq_v, gk_v, gv_v, gw_v,
    q, k, v, c, wall, dn,
    a_send, a_recv, p_send, prior,
    b_send, b_recv, l_send, later,
    attend, part, normed, dmixed, n_send, nall, ccolt,
    gk_part, gv_part, g_tile, g_rows, g_send, g_recv, g_out, g_in,
    load_sem, send_sem, a_sem, p_sem, b_sem, l_sem, g_sem,
    w_sem, c_sem, n_sem, swap_sem,
):
    dps, ny, nz, heads = sizes
    nx = dps // 2
    seqs = ny * nz
    block = q.shape[0]
    half = block // 2
    me_dp, me = lax.axis_index("dp"), lax.axis_index("seq")
    x, core = me_dp // 2, me_dp % 2
    y, z = me // nz, me % nz
    x_right, x_left, x_opposite = (x + 1) % nx, (x + nx - 1) % nx, (x + 2) % nx
    other = 1 - core
    right, left, opposite = x_right * 2 + core, x_left * 2 + core, x_opposite * 2 + core
    sibling = x * 2 + other
    right_s, left_s, opposite_s = x_right * 2 + other, x_left * 2 + other, x_opposite * 2 + other

    rows = [(y + d) % ny for d in range(ny)]
    columns = [(z + d) % nz for d in range(nz)]
    others = far_first(ny, nz)[:-1]
    mine = z * ny + y
    near_columns = sorted(range(nz), key=lambda d: apart(d, nz))
    halves = (near_columns[: nz - 2], near_columns[nz - 2 :])

    loads = [
        pltpu.make_async_copy(src, dst, load_sem.at[i])
        for i, (src, dst) in enumerate(
            [(k_hbm, k), (v_hbm, v), (w_hbm, wall.at[me_dp]), (q_hbm, q), (c_hbm, c)]
        )
    ]
    for load in loads:
        load.start()

    barrier = pltpu.get_barrier_semaphore()

    def greet(dp, seq):
        pl.semaphore_signal(barrier, inc=1, device_id=(dp, seq), device_id_type=MESH)

    for dy, dz in others:
        greet(me_dp, rows[dy] * nz + columns[dz])
    for dp in (opposite, opposite_s, right, left, right_s, left_s, sibling):
        greet(dp, me)

    loads[0].wait()
    loads[1].wait()
    for h in range(heads):
        cols = slice(h * DH, (h + 1) * DH)
        a_send[h * 8 : h * 8 + 8] = dot(k[:, cols], v[:, cols], (0, 0)).astype(BF16).reshape(8, 16, DH)
    a_recv[me] = a_send[mine]
    loads[2].wait()
    pl.semaphore_wait(barrier, seqs - 1 + dps - 1)

    def remote(src, dst, send, recv, dp, seq):
        return pltpu.make_async_remote_copy(
            src_ref=src, dst_ref=dst, send_sem=send, recv_sem=recv, device_id=(dp, seq), device_id_type=MESH
        )

    def send(ref, group, recv, dp):
        remote(ref, ref, send_sem.at[group], recv, dp, me).start()

    def arrived(ref, sem):
        remote(ref, ref, send_sem.at[0], sem, sibling, me).wait_recv()

    def to_owners(source, landing, group, recv, offsets):
        for dy, dz in offsets:
            row, column = rows[dy], columns[dz]
            piece = source.at[column * ny + row]
            remote(piece, landing.at[me], send_sem.at[group], recv, me_dp, row * nz + column).start()

    def give_back(source, landing, slot, group, recv):
        for dy, dz in others:
            seq = rows[dy] * nz + columns[dz]
            remote(source.at[seq], landing.at[slot], send_sem.at[group], recv, me_dp, seq).start()

    def given_back(landing, dz, recv):
        count = ny - 1 if dz == 0 else ny
        arrived(landing.at[pl.ds(0, count)], recv.at[columns[dz]])

    W_LEFT0, W_LEFT1, W_RIGHT0, W_RIGHT1, W_OPP0, W_OPP1, W_SIB, W_SIB_LEFT, W_SIB_RIGHT, W_SIB_OPP = range(10)
    low, high = pl.ds(0, half), pl.ds(half, half)
    send(wall.at[me_dp, low], 0, w_sem.at[W_LEFT0], right)
    send(wall.at[me_dp, high], 0, w_sem.at[W_RIGHT1], left)
    to_owners(a_send, a_recv, 1, a_sem, others)
    send(wall.at[me_dp, high], 0, w_sem.at[W_LEFT1], right)
    send(wall.at[me_dp, low], 0, w_sem.at[W_RIGHT0], left)
    send(wall.at[me_dp], 0, w_sem.at[W_SIB], sibling)

    loads[3].wait()
    causal = lax.broadcasted_iota(jnp.int32, (block, block), 0) >= lax.broadcasted_iota(
        jnp.int32, (block, block), 1
    )
    for h in range(heads):
        cols = slice(h * DH, (h + 1) * DH)
        near = jnp.where(causal, dot(q[:, cols], k[:, cols], (1, 1)), 0.0).astype(BF16)
        attend[h] = near
        part[h] = dot(near, v[:, cols], (1, 0))

    arrived(wall.at[left, low], w_sem.at[W_LEFT0])
    send(wall.at[left, low], 0, w_sem.at[W_OPP0], right)
    arrived(wall.at[right, high], w_sem.at[W_RIGHT1])
    send(wall.at[right, high], 0, w_sem.at[W_OPP1], left)

    loads[4].wait()
    own_c = ccolt.at[:, head_cols(me_dp)]
    for h in range(heads):
        rows_h = slice(h * DH, (h + 1) * DH)
        g_tile[rows_h, :] = c[:, rows_h].astype(F32).T
        for r in range(2):
            g_rows[pl.ds(2 * h + r, seqs, stride=16), :] = g_tile[pl.ds(h * DH + r, seqs, stride=2), :]
    ccolt[:, head_cols(me_dp)] = g_rows[...].astype(BF16)
    C_LEFT, C_RIGHT, C_OPP, C_SIB, C_SIB_LEFT, C_SIB_RIGHT, C_SIB_OPP = range(7)
    send(own_c, 2, c_sem.at[C_LEFT], right)
    send(own_c, 2, c_sem.at[C_RIGHT], left)
    send(own_c, 2, c_sem.at[C_OPP], opposite)
    send(own_c, 2, c_sem.at[C_SIB], sibling)

    arrived(a_recv.at[pl.ds(0, seqs - 1)], a_sem)

    def forward_sum(s, total):
        p_send[s] = total.astype(BF16)
        return total + a_recv[s].astype(F32)

    lax.fori_loop(0, seqs, forward_sum, jnp.zeros((16, DH), F32), unroll=8)
    prior[mine] = p_send[me]
    give_back(p_send, prior, mine, 3, p_sem.at[z])

    arrived(wall.at[left, high], w_sem.at[W_LEFT1])
    send(wall.at[left], 0, w_sem.at[W_SIB_LEFT], sibling)
    arrived(wall.at[right, low], w_sem.at[W_RIGHT0])
    send(wall.at[right], 0, w_sem.at[W_SIB_RIGHT], sibling)
    arrived(wall.at[opposite, low], w_sem.at[W_OPP0])
    arrived(wall.at[opposite, high], w_sem.at[W_OPP1])
    send(wall.at[opposite], 0, w_sem.at[W_SIB_OPP], sibling)

    arrived(wall.at[sibling], w_sem.at[W_SIB])
    arrived(wall.at[left_s], w_sem.at[W_SIB_LEFT])
    arrived(wall.at[right_s], w_sem.at[W_SIB_RIGHT])
    arrived(wall.at[opposite_s], w_sem.at[W_SIB_OPP])
    dn[...] = dot(c[...], wall[...].reshape(dps * block, heads * DH), (1, 0))

    for half_dz in halves:
        group = [columns[dz] for dz in half_dz]
        for dz in half_dz:
            given_back(prior, dz, p_sem)
        kept = []
        for h in group:
            mixed = part[h] + dot(q[:, head_cols(h)], prior[pl.ds(h * 8, 8)].reshape(DH, DH), (1, 0))
            inverse = lax.rsqrt(jnp.mean(mixed * mixed, axis=-1, keepdims=True) + EPSILON)
            n = mixed * inverse
            n_send[h] = n.astype(BF16)
            kept.append((n, inverse))
        for h, (n, inverse) in zip(group, kept):
            dnormed = dn[:, head_cols(h)]
            dmix = (dnormed - n * jnp.mean(dnormed * n, axis=-1, keepdims=True)) * inverse
            dmix = dmix.astype(BF16)
            u = dot(q[:, head_cols(h)], dmix, (0, 0))
            b_send[pl.ds(h * 8, 8)] = u.astype(BF16).reshape(8, 16, DH)
            dmixed[h] = dmix
            normed[:, head_cols(h)] = n.astype(BF16)
        to_owners(b_send, b_recv, 4, b_sem, [o for o in others if o[1] in half_dz])
        for h in group:
            @pl.when(h != me_dp)
            def _(h=h):
                remote(n_send.at[h], nall.at[me_dp], send_sem.at[5], n_sem, h, me).start()

    b_recv[me] = b_send[mine]
    nall[me_dp] = n_send[me_dp]

    for dp, here, there in ((left, C_LEFT, C_SIB_LEFT), (right, C_RIGHT, C_SIB_RIGHT), (opposite, C_OPP, C_SIB_OPP)):
        tokens = ccolt.at[:, head_cols(dp)]
        arrived(tokens, c_sem.at[here])
        send(tokens, 2, c_sem.at[there], sibling)

    for dp, there in ((sibling, C_SIB), (left_s, C_SIB_LEFT), (right_s, C_SIB_RIGHT), (opposite_s, C_SIB_OPP)):
        arrived(ccolt.at[:, head_cols(dp)], c_sem.at[there])
    arrived(nall.at[pl.ds(0, dps - 1)], n_sem)
    factor = 1.0 / math.sqrt(dps * block * seqs)
    g = dot(ccolt[...], nall[...].reshape(dps * block, DH), (1, 0)) * factor
    g_send[...] = g.astype(BF16).reshape(seqs, 16, DH)
    g_recv[me] = g_send[me]

    def sum_back():
        arrived(b_recv.at[pl.ds(0, seqs - 1)], b_sem)

        def backward_sum(i, total):
            s = seqs - 1 - i
            l_send[s] = total.astype(BF16)
            return total + b_recv[s].astype(F32)

        lax.fori_loop(0, seqs, backward_sum, jnp.zeros((16, DH), F32), unroll=8)
        later[mine] = l_send[me]
        give_back(l_send, later, mine, 6, l_sem.at[z])

    give_back(g_send, g_recv, me, 7, g_sem)
    sum_back()

    for h in range(heads):
        cols = slice(h * DH, (h + 1) * DH)
        dmix = dmixed[h]
        back = jnp.where(causal, dot(dmix, v[:, cols], (1, 1)), 0.0).astype(BF16)
        grad_q = dot(back, k[:, cols], (1, 0)) + dot(dmix, prior[h * 8 : h * 8 + 8].reshape(DH, DH), (1, 1))
        gq_v[:, cols] = grad_q.astype(BF16)
        gk_part[h] = dot(back, q[:, cols], (0, 0))
        gv_part[h] = dot(attend[h], dmix, (0, 0))

    for d in range(dps):
        out_v[:, d * DH : (d + 1) * DH] = dot(normed[...], wall[d], (1, 1)).astype(BF16)

    arrived(g_recv.at[pl.ds(0, seqs - 1)], g_sem)
    total = lax.fori_loop(0, seqs, lambda s, t: t + g_recv[s].astype(F32), jnp.zeros((16, DH), F32), unroll=8)
    for d in range(dps):
        g_out[d] = total[2 * d : 2 * d + 2]
    g_in[me_dp] = g_out[me_dp]
    for dp in (opposite, opposite_s, right, right_s, left, left_s, sibling):
        remote(g_out.at[dp], g_in.at[me_dp], send_sem.at[8], swap_sem, dp, me).start()

    for half_dz in halves:
        for dz in half_dz:
            given_back(later, dz, l_sem)
        for dz in half_dz:
            h = columns[dz]
            cols = head_cols(h)
            state = later[pl.ds(h * 8, 8)].reshape(DH, DH)
            gk_v[:, cols] = (gk_part[h] + dot(v[:, cols], state, (1, 1))).astype(BF16)
            gv_v[:, cols] = (gv_part[h] + dot(k[:, cols], state, (1, 0))).astype(BF16)

    def sent(ref, i):
        remote(ref, ref, send_sem.at[i], a_sem, sibling, me).wait_send()

    sent(wall.at[pl.ds(0, 7)], 0)
    sent(a_send.at[pl.ds(0, seqs - 1)], 1)
    sent(ccolt.at[:, pl.ds(0, 7 * block)], 2)
    sent(p_send.at[pl.ds(0, seqs - 1)], 3)
    sent(b_send.at[pl.ds(0, seqs - 1)], 4)
    sent(nall.at[pl.ds(0, dps - 1)], 5)
    sent(l_send.at[pl.ds(0, seqs - 1)], 6)

    sent(g_send.at[pl.ds(0, seqs - 1)], 7)
    sent(g_out.at[pl.ds(0, dps - 1)], 8)
    arrived(g_in.at[pl.ds(0, dps - 1)], swap_sem)
    for d in range(dps):
        gw_v[:, d * DH : (d + 1) * DH] = g_in[d]


def place(*refs):
    count = len(refs) // 2
    sems = refs[-1]
    copies = [pltpu.make_async_copy(refs[i], refs[count + i], sems.at[i]) for i in range(count)]
    for copy in copies:
        copy.start()
    for copy in copies:
        copy.wait()


def local(sizes, queries, keys, values, cotangent, out_weight):
    dps, ny, nz, heads = sizes
    _, block, features = queries.shape
    seqs = ny * nz
    shapes = [jax.ShapeDtypeStruct((block, features), BF16)] * 4 + [jax.ShapeDtypeStruct((2, features), F32)]
    arguments = (queries[0], keys[0], values[0], cotangent[0], out_weight)
    states = pltpu.VMEM((seqs, 16, DH), BF16)
    whole = pltpu.VMEM((block, features), BF16)
    per_head = pltpu.VMEM((heads, block, DH), F32)
    dma = pltpu.SemaphoreType.DMA
    piece = pltpu.VMEM((dps, 2, DH), F32)
    out = pl.pallas_call(
        functools.partial(kernel, sizes),
        out_shape=[pltpu.VMEM(s.shape, s.dtype) for s in shapes],
        in_specs=[pl.BlockSpec(memory_space=pl.ANY)] * 5,
        out_specs=[pl.BlockSpec(memory_space=pltpu.VMEM)] * 5,
        scratch_shapes=[
            whole, whole, whole, whole,
            pltpu.VMEM((dps, block, features), BF16),
            pltpu.VMEM((block, features), F32),
            states, states, states, states,
            states, states, states, states,
            pltpu.VMEM((heads, block, block), BF16),
            per_head,
            whole,
            pltpu.VMEM((heads, block, DH), BF16),
            pltpu.VMEM((heads, block, DH), BF16),
            pltpu.VMEM((dps, block, DH), BF16),
            pltpu.VMEM((features, dps * block), BF16),
            per_head, per_head,
            pltpu.VMEM((features, DH), F32),
            pltpu.VMEM((seqs * 16, DH), F32),
            states, states, piece, piece,
            dma((5,)), dma((9,)), dma, dma((heads,)), dma, dma((heads,)), dma,
            dma((10,)), dma((7,)), dma, dma,
        ],
        compiler_params=pltpu.CompilerParams(
            collective_id=0, has_side_effects=True, vmem_limit_bytes=VMEM_LIMIT
        ),
        name="layer",
    )(*(pltpu.with_memory_space_constraint(a, pltpu.HBM) for a in arguments))
    out = pl.pallas_call(
        place,
        out_shape=shapes,
        in_specs=[pl.BlockSpec(memory_space=pl.ANY)] * 5,
        out_specs=[pl.BlockSpec(memory_space=pl.ANY)] * 5,
        scratch_shapes=[dma((5,))],
        compiler_params=pltpu.CompilerParams(vmem_limit_bytes=VMEM_LIMIT),
        name="place",
    )(*out)
    return tuple(part[None] for part in out[:4]) + (out[4],)


def solution(mesh):
    seqs = mesh.shape["seq"]
    ny = nz = math.isqrt(seqs)
    sizes = (mesh.shape["dp"], ny, nz, 8)
    tokens = P("dp", "seq", None)
    return jax.shard_map(
        functools.partial(local, sizes),
        mesh=mesh,
        in_specs=(tokens, tokens, tokens, tokens, P("dp", None)),
        out_specs=(tokens, tokens, tokens, tokens, P(("dp", "seq"), None)),
        check_vma=False,
    )
```
